512 devices in a mesh: ctx: 64 (over z, x, core), head: 8 (over y).
Axes of the slice: x: 4, y: 8, z: 8, core: 2. Of those that a mesh axis runs over, the one named last changes fastest.
Arguments:
- tokens: bfloat16 [2, 16, 8192], P(None, None, 'ctx'), may hold values from -6 to 6
- w_query: bfloat16 [8192, 8192], P('ctx', 'head'), may hold values from -0.0625 to 0.0625
- w_key: bfloat16 [8192, 1024], P('ctx', 'head'), may hold values from -0.5 to 0.5
- w_value: bfloat16 [8192, 1024], P('ctx', 'head'), may hold values from -0.125 to 0.125
- key_cache: bfloat16 [2, 8, 131072, 128], P(None, 'head', 'ctx'), may hold values from -180 to 180
- value_cache: bfloat16 [2, 8, 131072, 128], P(None, 'head', 'ctx'), may hold values from -6 to 6
- lengths: int32 [2], replicated, may hold values from 65536 to 131072, as said below
- w_out: bfloat16 [8192, 8192], P('head', 'ctx'), may hold values from -0.1875 to 0.1875
Outputs:
- mixed: bfloat16 [2, 16, 8192], P(None, None, ('ctx', 'head'))
The draws below stay inside these ranges and needn't reach their ends.
Inputs may be any that keep to these rules, and one draw needn't show every extreme that they name: `lengths`: every row's length is at least 65536, and one row's is exactly 131072.
All inputs are finite; a program needn't handle non-finite values.
Results may differ from the reference program's by a relative error of at most 0.015.
The reference program's roundings to bfloat16 on the way (of `query` and `attended`) count: a program that leaves them out, or rounds other values in their place, can miss the bound.
Values may be sent and summed in bfloat16 or wider, within the bound.
A program may use at most 64 MiB of HBM per device.

```python
import math
import jax
import jax.numpy as jnp
from jax import lax

D = 8192
DH = 128
QPK = 8
KVH = 8
HEADS = 64
ROWS = 2
QLEN = 16
CTX_DEV = 2048
CONTEXT = 131072
N_HEAD = 8


def draw_lengths(key, part):
    key = jax.random.fold_in(key, 11)
    first_key, second_key = jax.random.split(key)
    full_row = jax.random.randint(first_key, (), 0, ROWS)
    others = jax.random.randint(second_key, (ROWS,), CONTEXT // 2, CONTEXT + 1)
    return jnp.where(jnp.arange(ROWS) == full_row, CONTEXT, others).astype(jnp.int32)


def draw_key_cache(key, part):
    key = jax.random.fold_in(key, 23)
    first_key = jax.random.fold_in(key, 0)
    fourth_key = jax.random.fold_in(key, 3)
    base = jnp.clip(jax.random.normal(first_key, (ROWS, KVH, CONTEXT, DH), jnp.float32), -3.0, 3.0)
    block_count = 2 * CONTEXT // CTX_DEV
    level = jnp.exp(jax.random.uniform(fourth_key, (ROWS, KVH, block_count, 1), jnp.float32, jnp.log(0.5), 0.0))
    level = jnp.repeat(level, CTX_DEV // 2, axis=2)
    scaled = base * 3.0 * level
    return scaled.astype(jnp.bfloat16)


def block_scale(own_key, extent, shards, smallest, top_value):
    def one(axis_at, shards_of):
        draws = jax.random.uniform(jax.random.fold_in(jax.random.fold_in(own_key, 6), axis_at), (shards_of,), jnp.float32, smallest / len(shards), top_value / len(shards))
        return jnp.repeat(jnp.exp(draws), extent[axis_at] // shards_of).reshape((-1,) + (1,) * (len(extent) - axis_at - 1))

    gain = one(*shards[0])
    for cut in shards[1:]:
        gain = gain * one(*cut)
    return gain


def noise(key, dims, deviation, most, cuts=(), kind=jnp.bfloat16):
    level = block_scale(key, dims, cuts, -0.22, 0.18) if cuts else 1.0
    drawn = jax.random.normal(key, dims, jnp.float32) * deviation * level
    return jnp.minimum(jnp.maximum(drawn, -most), most).astype(kind)


def setup_inputs(seed: int = 0) -> dict:
    seeds = jax.random.split(jax.random.key(seed), 9)
    tokens = noise(seeds[0], (ROWS, QLEN, D), 1.0, 6.0, ((2, 64),))
    w_query = noise(seeds[1], (D, HEADS * DH), D ** -0.5, 0.0625, ((0, 64), (1, 8)))
    w_key = noise(seeds[2], (D, KVH * DH), (D // 64) ** -0.5, 0.5, ((0, 64), (1, 8)))
    w_value = noise(seeds[3], (D, KVH * DH), (D // 4) ** -0.5, 0.125, ((0, 64), (1, 8)))
    key_cache = draw_key_cache(jax.random.fold_in(seeds[8], 71), 0)
    value_cache = noise(seeds[5], (ROWS, KVH, CONTEXT, DH), 1.0, 6.0, ((1, 8), (2, 64)))
    lengths = draw_lengths(jax.random.fold_in(seeds[8], 71), 0)
    w_out = noise(seeds[7], (HEADS * DH, D), (DH * QPK) ** -0.5, 0.1875, ((0, 8), (1, 64)))
    return dict(tokens=tokens, w_query=w_query, w_key=w_key, w_value=w_value, key_cache=key_cache, value_cache=value_cache, lengths=lengths, w_out=w_out)


def reference(tokens, w_query, w_key, w_value, key_cache, value_cache, lengths, w_out):
    row_count, draft_count, model_width = tokens.shape
    kv_heads = key_cache.shape[1]
    context_len = key_cache.shape[2]
    head_dim = key_cache.shape[3]
    group_size = w_query.shape[1] // (kv_heads * head_dim)
    score_scale = 1.0 / math.sqrt(head_dim)
    flattened = tokens.reshape(row_count * draft_count, model_width)
    query = (jnp.dot(flattened, w_query, preferred_element_type=jnp.float32) * score_scale).astype(jnp.bfloat16)
    query = query.reshape(row_count, draft_count, kv_heads, group_size, head_dim)
    new_key = jnp.dot(flattened, w_key, preferred_element_type=jnp.float32)
    new_key = new_key.reshape(row_count, draft_count, kv_heads, head_dim)
    new_value = jnp.dot(flattened, w_value, preferred_element_type=jnp.float32)
    new_value = new_value.reshape(row_count, draft_count, kv_heads, head_dim)
    token_of_row = jnp.arange(group_size * draft_count, dtype=jnp.int32) % draft_count
    causal_mask = jnp.arange(draft_count, dtype=jnp.int32)[None, :] <= token_of_row[:, None]

    def one_pair(pair_index):
        row_index = pair_index // kv_heads
        kv_index = pair_index % kv_heads
        query_block = query[row_index, :, kv_index]
        query_block = query_block.transpose(1, 0, 2).reshape(group_size * draft_count, head_dim)
        key_block = key_cache[row_index, kv_index]
        cache_scores = jnp.dot(query_block, key_block.T, preferred_element_type=jnp.float32)
        is_live = jnp.arange(context_len, dtype=jnp.int32) < lengths[row_index]
        cache_scores = jnp.where(is_live[None, :], cache_scores, -jnp.inf)
        draft_scores = jnp.dot(query_block.astype(jnp.float32), new_key[row_index, :, kv_index].T, precision=lax.Precision.HIGHEST)
        draft_scores = jnp.where(causal_mask, draft_scores, -jnp.inf)
        top_score = jnp.maximum(cache_scores.max(axis=1), draft_scores.max(axis=1))
        cache_weights = jnp.exp(cache_scores - top_score[:, None])
        draft_weights = jnp.exp(draft_scores - top_score[:, None])
        denominator = cache_weights.sum(axis=1) + draft_weights.sum(axis=1)
        numerator = jnp.dot(cache_weights, value_cache[row_index, kv_index].astype(jnp.float32), precision=lax.Precision.HIGHEST)
        numerator = numerator + jnp.dot(draft_weights, new_value[row_index, :, kv_index], precision=lax.Precision.HIGHEST)
        result = (numerator / denominator[:, None]).astype(jnp.bfloat16)
        return result.reshape(group_size, draft_count, head_dim)
    results = lax.map(one_pair, jnp.arange(row_count * kv_heads, dtype=jnp.int32))
    attended = results.reshape(row_count, kv_heads, group_size, draft_count, head_dim)
    attended = attended.transpose(0, 3, 1, 2, 4).reshape(row_count * draft_count, kv_heads * group_size * head_dim)
    group_width = kv_heads // N_HEAD * group_size * head_dim
    total = jnp.zeros((row_count * draft_count, model_width), jnp.float32)
    for group_index in range(N_HEAD):
        lo = group_index * group_width
        partial_value = jnp.dot(attended[:, lo:lo + group_width], w_out[lo:lo + group_width], preferred_element_type=jnp.float32)
        rounded = lax.optimization_barrier(partial_value.astype(jnp.bfloat16))
        total = total + rounded.astype(jnp.float32)
    return total.astype(jnp.bfloat16).reshape(row_count, draft_count, model_width)
```

```python
import functools
import math

import jax
import jax.numpy as jnp
from jax import lax
from jax.experimental import pallas as pl
from jax.experimental.pallas import tpu as pltpu
from jax.sharding import PartitionSpec as P

F32, BF16 = jnp.float32, jnp.bfloat16
MESH = pl.DeviceIdType.MESH
NX = 4
NEG = -1e30


def dot_t(a, b, **kw):
    return lax.dot_general(a, b, (((1,), (1,)), ((), ())), preferred_element_type=F32, **kw)


def kernel(NZ, NY, slots,
           tok, wq, wk, wv, kc, vc, ln, wo, out,
           tok_v, wq_v, wk_v, wv_v, kc_v, vc_v, ln_s, wo_v, vt,
           p_other, p_own, r_core, s_x, r_x, s_z, r_zq, r_zkv, q_full, kv_full,
           s_buf, o_other, o_own, r_core2, s_x2, s_xml, r_x2, r_xml, s_z2, s_zml, r_z2, r_zml,
           o_draft, att, y_buf, s_y, r_y,
           load_sem, send_sem, recv_sem):
    ctx, y = lax.axis_index("ctx"), lax.axis_index("head")
    c = lax.rem(ctx, 2)
    x = lax.rem(ctx // 2, NX)
    z = ctx // (2 * NX)
    o = 1 - c

    def load(i, src, dst):
        cp = pltpu.make_async_copy(src, dst, load_sem.at[i])
        cp.start()
        return cp

    ld_tok = load(0, tok, tok_v)
    ld_wq = load(1, wq, wq_v)
    ld_wk = load(2, wk, wk_v)
    ld_wv = load(3, wv, wv_v)
    ld_vc = load(4, vc.at[:, 0], vc_v)
    ld_kc = load(5, kc.at[:, 0], kc_v)
    ld_wo = load(6, wo, wo_v)
    ld_ln = load(7, ln, ln_s)

    core_peer = {"ctx": ctx + 1 - 2 * c}
    x_peers = [(k, lax.rem(x + k, NX)) for k in (2, 1, 3)]
    x_dev = [{"ctx": (z * NX + xp) * 2 + c} for _, xp in x_peers]
    z_off = sorted(range(1, NZ), key=lambda k: -min(k, NZ - k))
    z_dev = [{"ctx": (lax.rem(z + k, NZ) * NX + x) * 2 + c} for k in z_off]
    y_off = sorted(range(1, NY), key=lambda k: -min(k, NY - k))
    y_dev = [{"head": lax.rem(y + k, NY)} for k in y_off]

    bar = pltpu.get_barrier_semaphore()
    everyone = z_dev + y_dev + x_dev + [core_peer]
    for d in everyone:
        pl.semaphore_signal(bar, inc=1, device_id=d, device_id_type=MESH)

    pending = []

    def send(ph, src, dst, dev):
        cp = pltpu.make_async_remote_copy(src_ref=src, dst_ref=dst, send_sem=send_sem.at[ph],
                                          recv_sem=recv_sem.at[ph], device_id=dev, device_id_type=MESH)
        cp.start()

    def arrive(ph, ref):
        pltpu.make_async_copy(ref, ref, recv_sem.at[ph]).wait()
        pending.append((ph, ref))

    def project(b, dst):
        t = tok_v[b]
        q = jnp.dot(t, wq_v[...], preferred_element_type=F32)
        k = jnp.dot(t, wk_v[...], preferred_element_type=F32)
        v = jnp.dot(t, wv_v[...], preferred_element_type=F32)
        for r in range(2):
            rows = slice(8 * r, 8 * r + 8)
            for ch, kv in ((0, k), (1, v)):
                dst[2 * r + ch, :, 0:512] = q[rows, 512 * ch:512 * ch + 512]
                dst[2 * r + ch, :, 512:640] = kv[rows]

    for cp in (ld_tok, ld_wq, ld_wk, ld_wv):
        cp.wait()
    project(o, p_other)
    pl.semaphore_wait(bar, len(everyone))
    send(0, p_other, r_core, core_peer)
    project(c, p_own)
    arrive(0, r_core)

    for i, (k, xp) in enumerate(x_peers):
        s_x[i] = p_own[xp] + r_core[xp]
        send(1, s_x.at[i], r_x.at[i], x_dev[i])
    mine = p_own[x] + r_core[x]
    arrive(1, r_x)
    for i in range(NX - 1):
        mine = mine + r_x[i]
    s_z[...] = mine
    for i in range(NZ - 1):
        send(2, s_z.at[:, 0:512], r_zq.at[i], z_dev[i])
    for i in range(NZ - 1):
        send(3, s_z.at[:, 512:640], r_zkv.at[i], z_dev[i])

    ld_vc.wait()
    for b in range(2):
        for i in range(4):
            vt[b, 0:128, 512 * i:512 * i + 512] = vc_v[b, 512 * i:512 * i + 512].T
        vt[b, 128:144] = jnp.ones((16, vt.shape[2]), BF16)
    ld_kc.wait()
    ld_ln.wait()

    qs = mine[:, 0:512]
    if NZ > 1:
        arrive(2, r_zq)
        for i in range(NZ - 1):
            qs = qs + r_zq[i]
    qs = jnp.concatenate([qs[:, 128 * i:128 * i + 128] for i in range(4)], axis=0)
    q_full[c, x] = (qs * (1.0 / math.sqrt(128.0))).astype(BF16)
    for i in range(NX - 1):
        send(4, q_full.at[c, x], q_full.at[c, x], x_dev[i])
    kvs = mine[:, 512:640]
    if NZ > 1:
        arrive(3, r_zkv)
        for i in range(NZ - 1):
            kvs = kvs + r_zkv[i]
    kv_full[x] = kvs
    for i in range(NX - 1):
        send(5, kv_full.at[x], kv_full.at[x], x_dev[i])
    arrive(4, q_full.at[0, 0:NX - 1])
    send(6, q_full.at[c], q_full.at[c], core_peer)
    arrive(6, q_full.at[0])

    n_pos = kc_v.shape[1]
    step = 512

    def attend(b, dst):
        q = q_full[b].reshape(128, 128)
        live = ln_s[b] - ctx * n_pos
        m = jnp.full((8, 128), NEG, F32)
        for i in range(n_pos // step):
            s = dot_t(kc_v[b, step * i:step * (i + 1)], q)
            at = lax.broadcasted_iota(jnp.int32, (step, 128), 0) + step * i
            s = jnp.where(at < live, s, NEG)
            s_buf[step * i:step * (i + 1)] = s
            m = jnp.maximum(m, jnp.max(s.reshape(step // 8, 8, 128), axis=0))
        m = jnp.max(m, axis=0, keepdims=True)
        acc = jnp.zeros((144, 128), F32)
        for i in range(n_pos // step):
            w = jnp.exp(s_buf[step * i:step * (i + 1)] - m).astype(BF16)
            acc = acc + jnp.dot(vt[b, :, step * i:step * (i + 1)], w, preferred_element_type=F32)
        dst[0:128] = acc[0:128]
        dst[128:129] = m
        dst[129:130] = acc[128:129]

    attend(o, o_other)
    send(7, o_other, r_core2, core_peer)
    attend(c, o_own)
    arrive(7, r_core2)

    m1, m2 = o_own[128:129], r_core2[128:129]
    top = jnp.maximum(m1, m2)
    f1, f2 = jnp.exp(m1 - top), jnp.exp(m2 - top)
    total = f1 * o_own[129:130] + f2 * r_core2[129:130]
    s_xml[0:1] = top
    s_xml[1:2] = total

    def chunk(xp):
        rows = pl.ds(pl.multiple_of(xp * 32, 32), 32)
        return f1 * o_own[rows] + f2 * r_core2[rows]

    for i, (k, xp) in enumerate(x_peers):
        s_x2[i] = chunk(xp).astype(BF16)
        send(8, s_x2.at[i], r_x2.at[i], x_dev[i])
        send(9, s_xml, r_xml.at[i], x_dev[i])
    part = chunk(x)

    arrive(5, kv_full.at[0:NX - 1])
    new_k = jnp.concatenate([kv_full[0], kv_full[2]], axis=0)
    new_v = jnp.concatenate([kv_full[1], kv_full[3]], axis=0)
    ds = dot_t(new_k, q_full[c].reshape(128, 128).astype(F32), precision=lax.Precision.HIGHEST)
    lane = lax.broadcasted_iota(jnp.int32, (16, 128), 1)
    u = lax.broadcasted_iota(jnp.int32, (16, 128), 0)
    ds = jnp.where(u <= (lane // 64) * 8 + lane % 8, ds, NEG)
    dm = jnp.max(ds, axis=0, keepdims=True)
    dw = jnp.exp(ds - dm)
    dl = jnp.sum(dw, axis=0, keepdims=True)
    o_draft[...] = lax.dot_general(new_v, dw, (((0,), (0,)), ((), ())), preferred_element_type=F32,
                                   precision=lax.Precision.HIGHEST)
    d_part = o_draft[pl.ds(pl.multiple_of(x * 32, 32), 32)]

    def combine(parts):
        top = functools.reduce(jnp.maximum, [m for m, _, _ in parts])
        tot, acc = 0.0, 0.0
        for m, l, a in parts:
            f = jnp.exp(m - top)
            tot = tot + f * l
            acc = acc + f * a
        return top, tot, acc

    arrive(8, r_x2)
    arrive(9, r_xml)
    top, total, part = combine(
        [(top, total, part)]
        + [(r_xml[i, 0:1], r_xml[i, 1:2], r_x2[i].astype(F32)) for i in range(NX - 1)])
    s_z2[...] = part.astype(BF16)
    s_zml[0:1] = top
    s_zml[1:2] = total
    for i in range(NZ - 1):
        send(10, s_z2, r_z2.at[i], z_dev[i])
        send(11, s_zml, r_zml.at[i], z_dev[i])
    ld_wo.wait()
    if NZ > 1:
        arrive(10, r_z2)
        arrive(11, r_zml)
    _, total, part = combine(
        [(top, total, part), (dm, dl, d_part)]
        + [(r_zml[i, 0:1], r_zml[i, 1:2], r_z2[i].astype(F32)) for i in range(NZ - 1)])
    att[c, x] = (part / total).astype(BF16)
    for i in range(NX - 1):
        send(12, att.at[c, x], att.at[c, x], x_dev[i])
    arrive(12, att.at[0, 0:NX - 1])
    send(13, att.at[c], att.at[c], core_peer)

    def mix(b):
        a = att[b].reshape(128, 128).astype(F32).T
        a = jnp.concatenate(
            [jnp.concatenate([a[64 * r + 8 * h:64 * r + 8 * h + 8] for h in range(8)], axis=1) for r in range(2)],
            axis=0)
        y_buf[b] = jnp.dot(a.astype(BF16), wo_v[...], preferred_element_type=F32)

    mix(c)
    arrive(13, att.at[0])
    mix(o)
    yt = y_buf[...].reshape(32, 128).T.astype(BF16)
    s_y[...] = yt.reshape(s_y.shape)
    for i in range(NY - 1):
        send(14, s_y.at[y_dev[i]["head"]], r_y.at[i], y_dev[i])
    ys = s_y[y].astype(F32)
    if NY > 1:
        arrive(14, r_y)
        for i in range(NY - 1):
            ys = ys + r_y[i].astype(F32)
    out[...] = ys.T.astype(BF16).reshape(out.shape)

    for ph, ref in pending:
        pltpu.make_async_copy(ref, ref, send_sem.at[ph]).wait()


def per_device(NZ, NY, *args):
    tok, wq, wk, wv, kc, vc, ln, wo = args
    n_pos, piece = kc.shape[2], wo.shape[1] // NY
    nz, ny = max(NZ - 1, 1), max(NY - 1, 1)
    V = pltpu.VMEM
    scratch = [
        V(tok.shape, BF16), V(wq.shape, BF16), V(wk.shape, BF16), V(wv.shape, BF16),
        V((2, n_pos, 128), BF16), V((2, n_pos, 128), BF16), pltpu.SMEM((2,), jnp.int32), V(wo.shape, BF16),
        V((2, 144, n_pos), BF16),
        V((4, 8, 640), F32), V((4, 8, 640), F32), V((4, 8, 640), F32),
        V((3, 8, 640), F32), V((3, 8, 640), F32), V((8, 640), F32), V((nz, 8, 512), F32), V((nz, 8, 128), F32),
        V((2, 4, 32, 128), BF16), V((4, 8, 128), F32),
        V((n_pos, 128), F32), V((136, 128), F32), V((136, 128), F32), V((136, 128), F32),
        V((3, 32, 128), BF16), V((2, 128), F32), V((3, 32, 128), BF16), V((3, 2, 128), F32),
        V((32, 128), BF16), V((2, 128), F32), V((nz, 32, 128), BF16), V((nz, 2, 128), F32),
        V((128, 128), F32), V((2, 4, 32, 128), BF16), V((2, 16, 128), F32),
        V((NY, piece, 32), BF16), V((ny, piece, 32), BF16),
        pltpu.SemaphoreType.DMA((8,)), pltpu.SemaphoreType.DMA((15,)), pltpu.SemaphoreType.DMA((15,)),
    ]
    return pl.pallas_call(
        functools.partial(kernel, NZ, NY, None),
        out_shape=jax.ShapeDtypeStruct((2, 16, piece), BF16),
        in_specs=[pl.BlockSpec(memory_space=pl.ANY)] * 8,
        out_specs=pl.BlockSpec(memory_space=pltpu.VMEM),
        scratch_shapes=scratch,
        compiler_params=pltpu.CompilerParams(
            collective_id=0, has_side_effects=True, vmem_limit_bytes=40 * 2**20),
        name="decode_step",
    )(*args)


def solution(mesh):
    NZ = mesh.shape["ctx"] // (2 * NX)
    return jax.shard_map(
        functools.partial(per_device, NZ, mesh.shape["head"]),
        mesh=mesh,
        in_specs=(
            P(None, None, "ctx"),
            P("ctx", "head"),
            P("ctx", "head"),
            P("ctx", "head"),
            P(None, "head", "ctx", None),
            P(None, "head", "ctx", None),
            P(),
            P("head", "ctx"),
        ),
        out_specs=P(None, None, ("ctx", "head")),
        check_vma=False,
    )
```

```python
import functools
import math

import jax
import jax.numpy as jnp
from jax import lax
from jax.experimental import pallas as pl
from jax.experimental.pallas import tpu as pltpu
from jax.sharding import PartitionSpec as P

F32, BF16 = jnp.float32, jnp.bfloat16
MESH = pl.DeviceIdType.MESH
NX = 4
NEG = -1e30


def dot_t(a, b, **kw):
    return lax.dot_general(a, b, (((1,), (1,)), ((), ())), preferred_element_type=F32, **kw)


def kernel(NZ, NY, slots,
           tok, wq, wk, wv, kc, vc, ln, wo, out,
           tok_v, wq_v, wk_v, wv_v, kc_v, vc_v, ln_s, wo_v, vt,
           p_other, p_own, r_core, s_x, r_x, s_z, r_zq, r_zkv, q_full, kv_full,
           s_buf, o_other, o_own, r_core2, s_x2, s_xml, r_x2, r_xml, s_z2, s_zml, r_z2, r_zml,
           o_draft, att, y_buf, s_y, r_y,
           load_sem, send_sem, recv_sem):
    ctx, y = lax.axis_index("ctx"), lax.axis_index("head")
    c = lax.rem(ctx, 2)
    x = lax.rem(ctx // 2, NX)
    z = ctx // (2 * NX)
    o = 1 - c

    core_peer = {"ctx": ctx + 1 - 2 * c}
    x_peers = [(k, lax.rem(x + k, NX)) for k in (2, 1, 3)]
    x_dev = [{"ctx": (z * NX + xp) * 2 + c} for _, xp in x_peers]
    z_off = sorted(range(1, NZ), key=lambda k: -min(k, NZ - k))
    z_dev = [{"ctx": (lax.rem(z + k, NZ) * NX + x) * 2 + c} for k in z_off]
    y_off = sorted(range(1, NY), key=lambda k: -min(k, NY - k))
    y_dev = [{"head": lax.rem(y + k, NY)} for k in y_off]

    bar = pltpu.get_barrier_semaphore()
    everyone = z_dev + y_dev + x_dev + [core_peer]
    for d in everyone:
        pl.semaphore_signal(bar, inc=1, device_id=d, device_id_type=MESH)

    def load(i, src, dst):
        cp = pltpu.make_async_copy(src, dst, load_sem.at[i])
        cp.start()
        return cp

    ld_tok = load(0, tok, tok_v)
    ld_wq = load(1, wq, wq_v)
    ld_wk = load(2, wk, wk_v)
    ld_wv = load(3, wv, wv_v)
    ld_vc = load(4, vc.at[:, 0], vc_v)
    ld_kc = load(5, kc.at[:, 0], kc_v)
    ld_wo = load(6, wo, wo_v)
    ld_ln = load(7, ln, ln_s)

    pending = []

    def send(ph, src, dst, dev):
        cp = pltpu.make_async_remote_copy(src_ref=src, dst_ref=dst, send_sem=send_sem.at[ph],
                                          recv_sem=recv_sem.at[ph], device_id=dev, device_id_type=MESH)
        cp.start()

    def arrive(ph, ref):
        pltpu.make_async_copy(ref, ref, recv_sem.at[ph]).wait()
        pending.append((ph, ref))

    def project(b, dst):
        t = tok_v[b]
        q = jnp.dot(t, wq_v[...], preferred_element_type=F32)
        k = jnp.dot(t, wk_v[...], preferred_element_type=F32)
        v = jnp.dot(t, wv_v[...], preferred_element_type=F32)
        for r in range(2):
            rows = slice(8 * r, 8 * r + 8)
            for ch, kv in ((0, k), (1, v)):
                dst[2 * r + ch, :, 0:512] = q[rows, 512 * ch:512 * ch + 512]
                dst[2 * r + ch, :, 512:640] = kv[rows]

    for cp in (ld_tok, ld_wq, ld_wk, ld_wv):
        cp.wait()
    project(o, p_other)
    pl.semaphore_wait(bar, len(everyone))
    send(0, p_other, r_core, core_peer)
    project(c, p_own)
    arrive(0, r_core)

    for i, (k, xp) in enumerate(x_peers):
        s_x[i] = p_own[xp] + r_core[xp]
        send(1, s_x.at[i], r_x.at[i], x_dev[i])
    mine = p_own[x] + r_core[x]
    arrive(1, r_x)
    for i in range(NX - 1):
        mine = mine + r_x[i]
    s_z[...] = mine
    for i in range(NZ - 1):
        send(2, s_z.at[:, 0:512], r_zq.at[i], z_dev[i])
    for i in range(NZ - 1):
        send(3, s_z.at[:, 512:640], r_zkv.at[i], z_dev[i])

    ld_vc.wait()
    for b in range(2):
        for i in range(4):
            vt[b, 0:128, 512 * i:512 * i + 512] = vc_v[b, 512 * i:512 * i + 512].T
        vt[b, 128:144] = jnp.ones((16, vt.shape[2]), BF16)
    ld_kc.wait()
    ld_ln.wait()

    qs = mine[:, 0:512]
    if NZ > 1:
        arrive(2, r_zq)
        for i in range(NZ - 1):
            qs = qs + r_zq[i]
    qs = jnp.concatenate([qs[:, 128 * i:128 * i + 128] for i in range(4)], axis=0)
    q_full[c, x] = (qs * (1.0 / math.sqrt(128.0))).astype(BF16)
    for i in range(NX - 1):
        send(4, q_full.at[c, x], q_full.at[c, x], x_dev[i])
    kvs = mine[:, 512:640]
    if NZ > 1:
        arrive(3, r_zkv)
        for i in range(NZ - 1):
            kvs = kvs + r_zkv[i]
    kv_full[x] = kvs
    for i in range(NX - 1):
        send(5, kv_full.at[x], kv_full.at[x], x_dev[i])
    arrive(4, q_full.at[0, 0:NX - 1])
    send(6, q_full.at[c], q_full.at[c], core_peer)
    arrive(6, q_full.at[0])

    n_pos = kc_v.shape[1]
    step = 512

    def attend(b, dst):
        q = q_full[b].reshape(128, 128)
        live = ln_s[b] - ctx * n_pos
        m = jnp.full((8, 128), NEG, F32)
        for i in range(n_pos // step):
            s = dot_t(kc_v[b, step * i:step * (i + 1)], q)
            at = lax.broadcasted_iota(jnp.int32, (step, 128), 0) + step * i
            s = jnp.where(at < live, s, NEG)
            s_buf[step * i:step * (i + 1)] = s
            m = jnp.maximum(m, jnp.max(s.reshape(step // 8, 8, 128), axis=0))
        m = jnp.max(m, axis=0, keepdims=True)
        acc = jnp.zeros((144, 128), F32)
        for i in range(n_pos // step):
            w = jnp.exp(s_buf[step * i:step * (i + 1)] - m).astype(BF16)
            acc = acc + jnp.dot(vt[b, :, step * i:step * (i + 1)], w, preferred_element_type=F32)
        dst[0:128] = acc[0:128]
        dst[128:129] = m
        dst[129:130] = acc[128:129]

    attend(o, o_other)
    send(7, o_other, r_core2, core_peer)
    attend(c, o_own)
    arrive(7, r_core2)

    m1, m2 = o_own[128:129], r_core2[128:129]
    top = jnp.maximum(m1, m2)
    f1, f2 = jnp.exp(m1 - top), jnp.exp(m2 - top)
    total = f1 * o_own[129:130] + f2 * r_core2[129:130]
    s_xml[0:1] = top
    s_xml[1:2] = total

    def chunk(xp):
        rows = pl.ds(pl.multiple_of(xp * 32, 32), 32)
        return f1 * o_own[rows] + f2 * r_core2[rows]

    for i, (k, xp) in enumerate(x_peers):
        s_x2[i] = chunk(xp).astype(BF16)
        send(8, s_x2.at[i], r_x2.at[i], x_dev[i])
        send(9, s_xml, r_xml.at[i], x_dev[i])
    part = chunk(x)

    arrive(5, kv_full.at[0:NX - 1])
    new_k = jnp.concatenate([kv_full[0], kv_full[2]], axis=0)
    new_v = jnp.concatenate([kv_full[1], kv_full[3]], axis=0)
    ds = dot_t(new_k, q_full[c].reshape(128, 128).astype(F32), precision=lax.Precision.HIGHEST)
    lane = lax.broadcasted_iota(jnp.int32, (16, 128), 1)
    u = lax.broadcasted_iota(jnp.int32, (16, 128), 0)
    ds = jnp.where(u <= (lane // 64) * 8 + lane % 8, ds, NEG)
    dm = jnp.max(ds, axis=0, keepdims=True)
    dw = jnp.exp(ds - dm)
    dl = jnp.sum(dw, axis=0, keepdims=True)
    o_draft[...] = lax.dot_general(new_v, dw, (((0,), (0,)), ((), ())), preferred_element_type=F32,
                                   precision=lax.Precision.HIGHEST)
    d_part = o_draft[pl.ds(pl.multiple_of(x * 32, 32), 32)]

    def combine(parts):
        top = functools.reduce(jnp.maximum, [m for m, _, _ in parts])
        tot, acc = 0.0, 0.0
        for m, l, a in parts:
            f = jnp.exp(m - top)
            tot = tot + f * l
            acc = acc + f * a
        return top, tot, acc

    arrive(8, r_x2)
    arrive(9, r_xml)
    top, total, part = combine(
        [(top, total, part)]
        + [(r_xml[i, 0:1], r_xml[i, 1:2], r_x2[i].astype(F32)) for i in range(NX - 1)])
    s_z2[...] = part.astype(BF16)
    s_zml[0:1] = top
    s_zml[1:2] = total
    for i in range(NZ - 1):
        send(10, s_z2, r_z2.at[i], z_dev[i])
        send(11, s_zml, r_zml.at[i], z_dev[i])
    ld_wo.wait()
    if NZ > 1:
        arrive(10, r_z2)
        arrive(11, r_zml)
    _, total, part = combine(
        [(top, total, part), (dm, dl, d_part)]
        + [(r_zml[i, 0:1], r_zml[i, 1:2], r_z2[i].astype(F32)) for i in range(NZ - 1)])
    att[c, x] = (part / total).astype(BF16)
    for i in range(NX - 1):
        send(12, att.at[c, x], att.at[c, x], x_dev[i])
    arrive(12, att.at[0, 0:NX - 1])
    send(13, att.at[c], att.at[c], core_peer)

    def mix(b):
        a = att[b].reshape(128, 128).astype(F32).T
        a = jnp.concatenate(
            [jnp.concatenate([a[64 * r + 8 * h:64 * r + 8 * h + 8] for h in range(8)], axis=1) for r in range(2)],
            axis=0)
        y_buf[b] = jnp.dot(a.astype(BF16), wo_v[...], preferred_element_type=F32)

    mix(c)
    arrive(13, att.at[0])
    mix(o)
    yt = y_buf[...].reshape(32, 128).T.astype(BF16)
    s_y[...] = yt.reshape(s_y.shape)
    for i in range(NY - 1):
        send(14, s_y.at[y_dev[i]["head"]], r_y.at[i], y_dev[i])
    ys = s_y[y].astype(F32)
    if NY > 1:
        arrive(14, r_y)
        for i in range(NY - 1):
            ys = ys + r_y[i].astype(F32)
    out[...] = ys.T.astype(BF16).reshape(out.shape)

    for ph, ref in pending:
        pltpu.make_async_copy(ref, ref, send_sem.at[ph]).wait()


def per_device(NZ, NY, *args):
    tok, wq, wk, wv, kc, vc, ln, wo = args
    n_pos, piece = kc.shape[2], wo.shape[1] // NY
    nz, ny = max(NZ - 1, 1), max(NY - 1, 1)
    V = pltpu.VMEM
    scratch = [
        V(tok.shape, BF16), V(wq.shape, BF16), V(wk.shape, BF16), V(wv.shape, BF16),
        V((2, n_pos, 128), BF16), V((2, n_pos, 128), BF16), pltpu.SMEM((2,), jnp.int32), V(wo.shape, BF16),
        V((2, 144, n_pos), BF16),
        V((4, 8, 640), F32), V((4, 8, 640), F32), V((4, 8, 640), F32),
        V((3, 8, 640), F32), V((3, 8, 640), F32), V((8, 640), F32), V((nz, 8, 512), F32), V((nz, 8, 128), F32),
        V((2, 4, 32, 128), BF16), V((4, 8, 128), F32),
        V((n_pos, 128), F32), V((136, 128), F32), V((136, 128), F32), V((136, 128), F32),
        V((3, 32, 128), BF16), V((2, 128), F32), V((3, 32, 128), BF16), V((3, 2, 128), F32),
        V((32, 128), BF16), V((2, 128), F32), V((nz, 32, 128), BF16), V((nz, 2, 128), F32),
        V((128, 128), F32), V((2, 4, 32, 128), BF16), V((2, 16, 128), F32),
        V((NY, piece, 32), BF16), V((ny, piece, 32), BF16),
        pltpu.SemaphoreType.DMA((8,)), pltpu.SemaphoreType.DMA((15,)), pltpu.SemaphoreType.DMA((15,)),
    ]
    return pl.pallas_call(
        functools.partial(kernel, NZ, NY, None),
        out_shape=jax.ShapeDtypeStruct((2, 16, piece), BF16),
        in_specs=[pl.BlockSpec(memory_space=pl.ANY)] * 8,
        out_specs=pl.BlockSpec(memory_space=pltpu.VMEM),
        scratch_shapes=scratch,
        compiler_params=pltpu.CompilerParams(
            collective_id=0, has_side_effects=True, vmem_limit_bytes=60 * 2**20),
        name="decode_step",
    )(*args)


def solution(mesh):
    NZ = mesh.shape["ctx"] // (2 * NX)
    return jax.shard_map(
        functools.partial(per_device, NZ, mesh.shape["head"]),
        mesh=mesh,
        in_specs=(
            P(None, None, "ctx"),
            P("ctx", "head"),
            P("ctx", "head"),
            P("ctx", "head"),
            P(None, "head", "ctx", None),
            P(None, "head", "ctx", None),
            P(),
            P("head", "ctx"),
        ),
        out_specs=P(None, None, ("ctx", "head")),
        check_vma=False,
    )
```

```python
import functools
import math

import jax
import jax.numpy as jnp
from jax import lax
from jax.experimental import pallas as pl
from jax.experimental.pallas import tpu as pltpu
from jax.sharding import PartitionSpec as P

F32, BF16 = jnp.float32, jnp.bfloat16
MESH = pl.DeviceIdType.MESH
NX = 4
NEG = -1e30


def dot_t(a, b, **kw):
    return lax.dot_general(a, b, (((1,), (1,)), ((), ())), preferred_element_type=F32, **kw)


def kernel(NZ, NY,
           tok, wq, wk, wv, kc, vc, ln, wo, out,
           tok_v, wq_v, wk_v, wv_v, k_v, v_v, ln_s, wo_v, vt,
           p_oq, p_okv, p_cq, p_ckv, r_cq, r_ckv, s_zq, r_zq, s_xkv, r_xkv, r_xq, s_zkv, r_zkv, q_full, kv_full,
           s_buf, o_buf, s_x2, s_xml, r_x2, r_xml, s_z2, s_zml, r_z2, r_zml,
           o_draft, att, y_buf, s_y, r_y,
           load_sem, send_sem, recv_sem):
    ctx, y = lax.axis_index("ctx"), lax.axis_index("head")
    c = lax.rem(ctx, 2)
    x = lax.rem(ctx // 2, NX)
    z = ctx // (2 * NX)
    o = 1 - c
    n_pos, hz = k_v.shape[1], 8 // NZ

    core_peer = {"ctx": ctx + 1 - 2 * c}
    x_peers = [lax.rem(x + k, NX) for k in (2, 1, 3)]
    x_dev = [{"ctx": (z * NX + xp) * 2 + c} for xp in x_peers]
    z_peers = [lax.rem(z + k, NZ) for k in sorted(range(1, NZ), key=lambda k: -min(k, NZ - k))]
    z_dev = [{"ctx": (zp * NX + x) * 2 + c} for zp in z_peers]
    y_peers = [lax.rem(y + k, NY) for k in sorted(range(1, NY), key=lambda k: -min(k, NY - k))]
    y_dev = [{"head": yp} for yp in y_peers]

    bar = pltpu.get_barrier_semaphore()
    everyone = z_dev + y_dev + x_dev + [core_peer]
    for d in everyone:
        pl.semaphore_signal(bar, inc=1, device_id=d, device_id_type=MESH)

    def load(i, src, dst):
        cp = pltpu.make_async_copy(src, dst, load_sem.at[i])
        cp.start()
        return cp

    ld_tok = load(0, tok, tok_v)
    ld_wq = load(1, wq, wq_v)
    ld_wk = load(2, wk, wk_v)
    ld_wv = load(3, wv, wv_v)
    ld_v = load(4, vc.at[c, 0], v_v.at[0])
    ld_k = load(5, kc.at[c, 0], k_v.at[0])
    ld_wo = load(6, wo, wo_v)
    ld_ln = load(7, ln, ln_s)

    pending = []

    def send(ph, src, dst, dev):
        pltpu.make_async_remote_copy(src_ref=src, dst_ref=dst, send_sem=send_sem.at[ph],
                                     recv_sem=recv_sem.at[ph], device_id=dev, device_id_type=MESH).start()

    def arrive(ph, ref):
        pltpu.make_async_copy(ref, ref, recv_sem.at[ph]).wait()
        pending.append((ph, ref))

    def project(b, dst_q, dst_kv):
        t = tok_v[b]
        q = jnp.dot(t, wq_v[...], preferred_element_type=F32)
        k = jnp.dot(t, wk_v[...], preferred_element_type=F32)
        v = jnp.dot(t, wv_v[...], preferred_element_type=F32)
        for h in range(8):
            dst_q[h] = q[:, 128 * h:128 * h + 128]
        for r in range(2):
            dst_kv[2 * r] = k[8 * r:8 * r + 8]
            dst_kv[2 * r + 1] = v[8 * r:8 * r + 8]

    for cp in (ld_tok, ld_wq, ld_wk, ld_wv):
        cp.wait()
    project(o, p_oq, p_okv)
    project(c, p_cq, p_ckv)
    pl.semaphore_wait(bar, len(everyone))
    send(0, p_oq, r_cq, core_peer)
    send(1, p_okv, r_ckv, core_peer)

    arrive(0, r_cq)
    for i, zp in enumerate(z_peers):
        heads = pl.ds(zp * hz, hz)
        s_zq[i] = p_cq[heads] + r_cq[heads]
        send(2, s_zq.at[i], r_zq.at[i], z_dev[i])
    heads = pl.ds(z * hz, hz)
    qs = p_cq[heads] + r_cq[heads]

    arrive(1, r_ckv)
    for i, xp in enumerate(x_peers):
        s_xkv[i] = p_ckv[xp] + r_ckv[xp]
        send(3, s_xkv.at[i], r_xkv.at[i], x_dev[i])
    kvs = p_ckv[x] + r_ckv[x]

    send(8, vc.at[o, 0], v_v.at[1], core_peer)
    send(9, kc.at[o, 0], k_v.at[1], core_peer)

    if NZ > 1:
        arrive(2, r_zq)
        for i in range(NZ - 1):
            qs = qs + r_zq[i]
    r_xq[x] = qs
    for i in range(NX - 1):
        send(4, r_xq.at[x], r_xq.at[x], x_dev[i])

    arrive(3, r_xkv)
    for i in range(NX - 1):
        kvs = kvs + r_xkv[i]
    s_zkv[...] = kvs
    for i in range(NZ - 1):
        send(5, s_zkv, r_zkv.at[i], z_dev[i])

    arrive(4, r_xq.at[0:NX - 1])
    qs = (r_xq[0] + r_xq[1]) + (r_xq[2] + r_xq[3])
    q_full[heads] = (qs * (1.0 / math.sqrt(128.0))).astype(BF16)
    for i in range(NZ - 1):
        send(6, q_full.at[heads], q_full.at[heads], z_dev[i])

    if NZ > 1:
        arrive(5, r_zkv)
        for i in range(NZ - 1):
            kvs = kvs + r_zkv[i]
    kv_full[x] = kvs
    for i in range(NX - 1):
        send(7, kv_full.at[x], kv_full.at[x], x_dev[i])

    vt[128:144] = jnp.ones((16, vt.shape[1]), BF16)

    def transpose_values(half):
        for i in range(4):
            w = n_pos // 4
            vt[0:128, half * n_pos + w * i:half * n_pos + w * (i + 1)] = v_v[half, w * i:w * (i + 1)].T

    ld_v.wait()
    transpose_values(0)
    arrive(8, v_v.at[0])
    transpose_values(1)
    ld_k.wait()
    arrive(9, k_v.at[0])
    ld_ln.wait()
    if NZ > 1:
        arrive(6, q_full.at[0:8 - hz])

    q = q_full[...].reshape(128, 128)
    step = 512
    steps = [(half, i) for half in range(2) for i in range(n_pos // step)]
    m = jnp.full((8, 128), NEG, F32)
    for n, (half, i) in enumerate(steps):
        s = dot_t(k_v[half, step * i:step * (i + 1)], q)
        live = ln_s[c] - (ctx + half * (1 - 2 * c)) * n_pos - step * i
        s = jnp.where(lax.broadcasted_iota(jnp.int32, (step, 128), 0) < live, s, NEG)
        s_buf[step * n:step * (n + 1)] = s
        m = jnp.maximum(m, jnp.max(s.reshape(step // 8, 8, 128), axis=0))
    m = jnp.max(m, axis=0, keepdims=True)
    acc = jnp.zeros((144, 128), F32)
    for n in range(len(steps)):
        w = jnp.exp(s_buf[step * n:step * (n + 1)] - m).astype(BF16)
        acc = acc + jnp.dot(vt[:, step * n:step * (n + 1)], w, preferred_element_type=F32)
    total = acc[128:129]
    o_buf[...] = acc[0:128]
    s_xml[0:1] = m
    s_xml[1:2] = total

    def chunk(xp):
        return o_buf[pl.ds(pl.multiple_of(xp * 32, 32), 32)]

    for i, xp in enumerate(x_peers):
        s_x2[i] = chunk(xp).astype(BF16)
        send(10, s_x2.at[i], r_x2.at[i], x_dev[i])
        send(11, s_xml, r_xml.at[i], x_dev[i])
    part = chunk(x)

    arrive(7, kv_full.at[0:NX - 1])
    new_k = jnp.concatenate([kv_full[0], kv_full[2]], axis=0)
    new_v = jnp.concatenate([kv_full[1], kv_full[3]], axis=0)
    ds = dot_t(new_k, q.astype(F32), precision=lax.Precision.HIGHEST)
    lane = lax.broadcasted_iota(jnp.int32, (16, 128), 1)
    u = lax.broadcasted_iota(jnp.int32, (16, 128), 0)
    ds = jnp.where(u <= lane % 16, ds, NEG)
    dm = jnp.max(ds, axis=0, keepdims=True)
    dw = jnp.exp(ds - dm)
    dl = jnp.sum(dw, axis=0, keepdims=True)
    o_draft[...] = lax.dot_general(new_v, dw, (((0,), (0,)), ((), ())), preferred_element_type=F32,
                                   precision=lax.Precision.HIGHEST)
    d_part = o_draft[pl.ds(pl.multiple_of(x * 32, 32), 32)]

    def combine(parts):
        top = functools.reduce(jnp.maximum, [m for m, _, _ in parts])
        tot, acc = 0.0, 0.0
        for m, l, a in parts:
            f = jnp.exp(m - top)
            tot = tot + f * l
            acc = acc + f * a
        return top, tot, acc

    arrive(10, r_x2)
    arrive(11, r_xml)
    m, total, part = combine(
        [(m, total, part)] + [(r_xml[i, 0:1], r_xml[i, 1:2], r_x2[i].astype(F32)) for i in range(NX - 1)])
    s_z2[...] = part.astype(BF16)
    s_zml[0:1] = m
    s_zml[1:2] = total
    for i in range(NZ - 1):
        send(12, s_z2, r_z2.at[i], z_dev[i])
        send(13, s_zml, r_zml.at[i], z_dev[i])
    ld_wo.wait()
    if NZ > 1:
        arrive(12, r_z2)
        arrive(13, r_zml)
    _, total, part = combine(
        [(m, total, part), (dm, dl, d_part)]
        + [(r_zml[i, 0:1], r_zml[i, 1:2], r_z2[i].astype(F32)) for i in range(NZ - 1)])
    att[c, x] = (part / total).astype(BF16)
    for i in range(NX - 1):
        send(14, att.at[c, x], att.at[c, x], x_dev[i])
    arrive(14, att.at[0, 0:NX - 1])
    send(15, att.at[c], att.at[c], core_peer)

    def mix(b):
        a = att[b].reshape(128, 128).T
        a = jnp.concatenate([a[16 * h:16 * h + 16] for h in range(8)], axis=1)
        y_buf[b] = jnp.dot(a, wo_v[...], preferred_element_type=F32)

    mix(c)
    arrive(15, att.at[0])
    mix(o)
    yt = y_buf[...].reshape(32, 128).T.astype(BF16)
    s_y[...] = yt.reshape(s_y.shape)
    for i in range(NY - 1):
        send(16, s_y.at[y_peers[i]], r_y.at[i], y_dev[i])
    ys = s_y[y].astype(F32)
    if NY > 1:
        arrive(16, r_y)
        for i in range(NY - 1):
            ys = ys + r_y[i].astype(F32)
    out[...] = ys.T.astype(BF16).reshape(out.shape)

    for ph, ref in pending:
        pltpu.make_async_copy(ref, ref, send_sem.at[ph]).wait()


def per_device(NZ, NY, *args):
    tok, wq, wk, wv, kc, vc, ln, wo = args
    n_pos, piece, hz = kc.shape[2], wo.shape[1] // NY, 8 // NZ
    nz, ny = max(NZ - 1, 1), max(NY - 1, 1)
    V = pltpu.VMEM
    scratch = [
        V(tok.shape, BF16), V(wq.shape, BF16), V(wk.shape, BF16), V(wv.shape, BF16),
        V((2, n_pos, 128), BF16), V((2, n_pos, 128), BF16), pltpu.SMEM((2,), jnp.int32), V(wo.shape, BF16),
        V((144, 2 * n_pos), BF16),
        V((8, 16, 128), F32), V((4, 8, 128), F32), V((8, 16, 128), F32), V((4, 8, 128), F32),
        V((8, 16, 128), F32), V((4, 8, 128), F32),
        V((nz, hz, 16, 128), F32), V((nz, hz, 16, 128), F32), V((3, 8, 128), F32), V((3, 8, 128), F32),
        V((4, hz, 16, 128), F32), V((8, 128), F32), V((nz, 8, 128), F32),
        V((8, 16, 128), BF16), V((4, 8, 128), F32),
        V((2 * n_pos, 128), F32), V((128, 128), F32),
        V((3, 32, 128), BF16), V((2, 128), F32), V((3, 32, 128), BF16), V((3, 2, 128), F32),
        V((32, 128), BF16), V((2, 128), F32), V((nz, 32, 128), BF16), V((nz, 2, 128), F32),
        V((128, 128), F32), V((2, 4, 32, 128), BF16), V((2, 16, 128), F32),
        V((NY, piece, 32), BF16), V((ny, piece, 32), BF16),
        pltpu.SemaphoreType.DMA((8,)), pltpu.SemaphoreType.DMA((17,)), pltpu.SemaphoreType.DMA((17,)),
    ]
    return pl.pallas_call(
        functools.partial(kernel, NZ, NY),
        out_shape=jax.ShapeDtypeStruct((2, 16, piece), BF16),
        in_specs=[pl.BlockSpec(memory_space=pl.ANY)] * 8,
        out_specs=pl.BlockSpec(memory_space=pltpu.VMEM),
        scratch_shapes=scratch,
        compiler_params=pltpu.CompilerParams(
            collective_id=0, has_side_effects=True, vmem_limit_bytes=60 * 2**20),
        name="decode_step",
    )(*args)


def solution(mesh):
    NZ = mesh.shape["ctx"] // (2 * NX)
    return jax.shard_map(
        functools.partial(per_device, NZ, mesh.shape["head"]),
        mesh=mesh,
        in_specs=(
            P(None, None, "ctx"),
            P("ctx", "head"),
            P("ctx", "head"),
            P("ctx", "head"),
            P(None, "head", "ctx", None),
            P(None, "head", "ctx", None),
            P(),
            P("head", "ctx"),
        ),
        out_specs=P(None, None, ("ctx", "head")),
        check_vma=False,
    )
```

```python
import functools
import math

import jax
import jax.numpy as jnp
from jax import lax
from jax.experimental import pallas as pl
from jax.experimental.pallas import tpu as pltpu
from jax.sharding import PartitionSpec as P

F32, BF16 = jnp.float32, jnp.bfloat16
MESH = pl.DeviceIdType.MESH
NX = 4
NEG = -1e30


def dot_t(a, b, **kw):
    return lax.dot_general(a, b, (((1,), (1,)), ((), ())), preferred_element_type=F32, **kw)


def kernel(NZ, NY,
           tok, wq, wk, wv, kc, vc, ln, wo, out,
           tok_v, wq_v, wk_v, wv_v, k_v, v_v, ln_s, wo_v, vt,
           p_oq, p_okv, p_cq, p_ckv, r_cq, r_ckv, s_zq, r_zq, s_xkv, r_xkv, r_xq, s_zkv, r_zkv, q_full, kv_full,
           s_buf, o_buf, s_x2, s_xml, r_x2, r_xml, s_z2, s_zml, r_z2, r_zml,
           o_draft, att, y_buf, s_y, r_y,
           load_sem, send_sem, recv_sem):
    ctx, y = lax.axis_index("ctx"), lax.axis_index("head")
    c = lax.rem(ctx, 2)
    x = lax.rem(ctx // 2, NX)
    z = ctx // (2 * NX)
    o = 1 - c
    n_pos, hz = k_v.shape[1], 8 // NZ

    core_peer = {"ctx": ctx + 1 - 2 * c}
    x_peers = [lax.rem(x + k, NX) for k in (2, 1, 3)]
    x_dev = [{"ctx": (z * NX + xp) * 2 + c} for xp in x_peers]
    far_dev = [{"ctx": (z * NX + xp) * 2 + o} for xp in x_peers]
    z_peers = [lax.rem(z + k, NZ) for k in sorted(range(1, NZ), key=lambda k: -min(k, NZ - k))]
    z_dev = [{"ctx": (zp * NX + x) * 2 + c} for zp in z_peers]
    y_peers = [lax.rem(y + k, NY) for k in sorted(range(1, NY), key=lambda k: -min(k, NY - k))]
    y_dev = [{"head": yp} for yp in y_peers]

    bar = pltpu.get_barrier_semaphore()
    everyone = z_dev + y_dev + far_dev + x_dev + [core_peer]
    for d in everyone:
        pl.semaphore_signal(bar, inc=1, device_id=d, device_id_type=MESH)

    def load(i, src, dst):
        cp = pltpu.make_async_copy(src, dst, load_sem.at[i])
        cp.start()
        return cp

    ld_tok = load(0, tok, tok_v)
    ld_wq = load(1, wq, wq_v)
    ld_wk = load(2, wk, wk_v)
    ld_wv = load(3, wv, wv_v)
    ld_v = load(4, vc.at[c, 0], v_v.at[0])
    ld_k = load(5, kc.at[c, 0], k_v.at[0])
    ld_wo = load(6, wo, wo_v)
    ld_ln = load(7, ln, ln_s)

    pending = []

    def send(ph, src, dst, dev):
        pltpu.make_async_remote_copy(src_ref=src, dst_ref=dst, send_sem=send_sem,
                                     recv_sem=recv_sem.at[ph], device_id=dev, device_id_type=MESH).start()

    def arrive(ph, ref):
        pltpu.make_async_copy(ref, ref, recv_sem.at[ph]).wait()
        pending.append(ref)

    def project(b, dst_q, dst_kv):
        t = tok_v[b]
        q = jnp.dot(t, wq_v[...], preferred_element_type=F32)
        k = jnp.dot(t, wk_v[...], preferred_element_type=F32)
        v = jnp.dot(t, wv_v[...], preferred_element_type=F32)
        for h in range(8):
            dst_q[h] = q[:, 128 * h:128 * h + 128]
        for r in range(2):
            dst_kv[2 * r] = k[8 * r:8 * r + 8]
            dst_kv[2 * r + 1] = v[8 * r:8 * r + 8]

    for cp in (ld_tok, ld_wq, ld_wk, ld_wv):
        cp.wait()
    project(o, p_oq, p_okv)
    project(c, p_cq, p_ckv)
    pl.semaphore_wait(bar, len(everyone))
    send(0, p_oq, r_cq, core_peer)
    send(1, p_okv, r_ckv, core_peer)

    arrive(0, r_cq)
    for i, zp in enumerate(z_peers):
        heads = pl.ds(zp * hz, hz)
        s_zq[i] = p_cq[heads] + r_cq[heads]
        send(2, s_zq.at[i], r_zq.at[i], z_dev[i])
    heads = pl.ds(z * hz, hz)
    qs = p_cq[heads] + r_cq[heads]

    arrive(1, r_ckv)
    for i, xp in enumerate(x_peers):
        s_xkv[i] = p_ckv[xp] + r_ckv[xp]
        send(3, s_xkv.at[i], r_xkv.at[i], x_dev[i])
    kvs = p_ckv[x] + r_ckv[x]

    send(8, vc.at[o, 0], v_v.at[1], core_peer)
    send(9, kc.at[o, 0], k_v.at[1], core_peer)

    if NZ > 1:
        arrive(2, r_zq)
        for i in range(NZ - 1):
            qs = qs + r_zq[i]
    r_xq[x] = qs
    for i in range(NX - 1):
        send(4, r_xq.at[x], r_xq.at[x], x_dev[i])

    arrive(3, r_xkv)
    for i in range(NX - 1):
        kvs = kvs + r_xkv[i]
    s_zkv[...] = kvs
    for i in range(NZ - 1):
        send(5, s_zkv, r_zkv.at[i], z_dev[i])

    arrive(4, r_xq.at[0:NX - 1])
    qs = (r_xq[0] + r_xq[1]) + (r_xq[2] + r_xq[3])
    q_full[heads] = (qs * (1.0 / math.sqrt(128.0))).astype(BF16)
    for i in range(NZ - 1):
        send(6, q_full.at[heads], q_full.at[heads], z_dev[i])

    if NZ > 1:
        arrive(5, r_zkv)
        for i in range(NZ - 1):
            kvs = kvs + r_zkv[i]
    kv_full[x] = kvs
    for i in range(NX - 1):
        send(7, kv_full.at[x], kv_full.at[x], x_dev[i])

    vt[128:144] = jnp.ones((16, vt.shape[1]), BF16)

    def transpose_values(half):
        for i in range(4):
            w = n_pos // 4
            vt[0:128, half * n_pos + w * i:half * n_pos + w * (i + 1)] = v_v[half, w * i:w * (i + 1)].T

    ld_v.wait()
    transpose_values(0)
    arrive(8, v_v.at[0])
    transpose_values(1)
    ld_k.wait()
    arrive(9, k_v.at[0])
    ld_ln.wait()
    if NZ > 1:
        arrive(6, q_full.at[0:8 - hz])

    q = q_full[...].reshape(128, 128)
    step = 512
    steps = [(half, i) for half in range(2) for i in range(n_pos // step)]
    m = jnp.full((8, 128), NEG, F32)
    for n, (half, i) in enumerate(steps):
        s = dot_t(k_v[half, step * i:step * (i + 1)], q)
        live = ln_s[c] - (ctx + half * (1 - 2 * c)) * n_pos - step * i
        s = jnp.where(lax.broadcasted_iota(jnp.int32, (step, 128), 0) < live, s, NEG)
        s_buf[step * n:step * (n + 1)] = s
        m = jnp.maximum(m, jnp.max(s.reshape(step // 8, 8, 128), axis=0))
    m = jnp.max(m, axis=0, keepdims=True)
    acc = jnp.zeros((144, 128), F32)
    for n in range(len(steps)):
        w = jnp.exp(s_buf[step * n:step * (n + 1)] - m).astype(BF16)
        acc = acc + jnp.dot(vt[:, step * n:step * (n + 1)], w, preferred_element_type=F32)
    total = acc[128:129]
    o_buf[...] = acc[0:128]
    s_xml[0:1] = m
    s_xml[1:2] = total
    def chunk(xp):
        return o_buf[pl.ds(pl.multiple_of(xp * 32, 32), 32)]

    for i, xp in enumerate(x_peers):
        s_x2[i] = chunk(xp).astype(BF16)
        send(10, s_x2.at[i], r_x2.at[i], x_dev[i])
        send(11, s_xml, r_xml.at[i], x_dev[i])
    part = chunk(x)

    arrive(7, kv_full.at[0:NX - 1])
    new_k = jnp.concatenate([kv_full[0], kv_full[2]], axis=0)
    new_v = jnp.concatenate([kv_full[1], kv_full[3]], axis=0)
    ds = dot_t(new_k, q.astype(F32), precision=lax.Precision.HIGHEST)
    lane = lax.broadcasted_iota(jnp.int32, (16, 128), 1)
    u = lax.broadcasted_iota(jnp.int32, (16, 128), 0)
    ds = jnp.where(u <= lane % 16, ds, NEG)
    dm = jnp.max(ds, axis=0, keepdims=True)
    dw = jnp.exp(ds - dm)
    dl = jnp.sum(dw, axis=0, keepdims=True)
    o_draft[...] = lax.dot_general(new_v, dw, (((0,), (0,)), ((), ())), preferred_element_type=F32,
                                   precision=lax.Precision.HIGHEST)
    d_part = o_draft[pl.ds(pl.multiple_of(x * 32, 32), 32)]

    def combine(parts):
        top = functools.reduce(jnp.maximum, [m for m, _, _ in parts])
        tot, acc = 0.0, 0.0
        for m, l, a in parts:
            f = jnp.exp(m - top)
            tot = tot + f * l
            acc = acc + f * a
        return top, tot, acc

    arrive(10, r_x2)
    arrive(11, r_xml)
    m, total, part = combine(
        [(m, total, part)] + [(r_xml[i, 0:1], r_xml[i, 1:2], r_x2[i].astype(F32)) for i in range(NX - 1)])
    s_z2[...] = part.astype(BF16)
    s_zml[0:1] = m
    s_zml[1:2] = total
    for i in range(NZ - 1):
        send(12, s_z2, r_z2.at[i], z_dev[i])
        send(13, s_zml, r_zml.at[i], z_dev[i])
    ld_wo.wait()
    if NZ > 1:
        arrive(12, r_z2)
        arrive(13, r_zml)
    _, total, part = combine(
        [(m, total, part), (dm, dl, d_part)]
        + [(r_zml[i, 0:1], r_zml[i, 1:2], r_z2[i].astype(F32)) for i in range(NZ - 1)])
    att[c, x] = (part / total).astype(BF16)
    for d in far_dev:
        send(15, att.at[c, x], att.at[c, x], d)
    for d in x_dev:
        send(14, att.at[c, x], att.at[c, x], d)
    send(15, att.at[c, x], att.at[c, x], core_peer)
    arrive(14, att.at[0, 0:NX - 1])

    def mix(b):
        a = att[b].reshape(128, 128).T
        a = jnp.concatenate([a[16 * h:16 * h + 16] for h in range(8)], axis=1)
        y_buf[b] = jnp.dot(a, wo_v[...], preferred_element_type=F32)

    mix(c)
    arrive(15, att.at[0])
    mix(o)
    yt = y_buf[...].reshape(32, 128).T.astype(BF16)
    s_y[...] = yt.reshape(s_y.shape)
    for i in range(NY - 1):
        send(16, s_y.at[y_peers[i]], r_y.at[i], y_dev[i])
    ys = s_y[y].astype(F32)
    if NY > 1:
        arrive(16, r_y)
        for i in range(NY - 1):
            ys = ys + r_y[i].astype(F32)
    out[...] = ys.T.astype(BF16).reshape(out.shape)

    for ref in pending:
        pltpu.make_async_copy(ref, ref, send_sem).wait()


def per_device(NZ, NY, *args):
    tok, wq, wk, wv, kc, vc, ln, wo = args
    n_pos, piece, hz = kc.shape[2], wo.shape[1] // NY, 8 // NZ
    nz, ny = max(NZ - 1, 1), max(NY - 1, 1)
    V = pltpu.VMEM
    scratch = [
        V(tok.shape, BF16), V(wq.shape, BF16), V(wk.shape, BF16), V(wv.shape, BF16),
        V((2, n_pos, 128), BF16), V((2, n_pos, 128), BF16), pltpu.SMEM((2,), jnp.int32), V(wo.shape, BF16),
        V((144, 2 * n_pos), BF16),
        V((8, 16, 128), F32), V((4, 8, 128), F32), V((8, 16, 128), F32), V((4, 8, 128), F32),
        V((8, 16, 128), F32), V((4, 8, 128), F32),
        V((nz, hz, 16, 128), F32), V((nz, hz, 16, 128), F32), V((3, 8, 128), F32), V((3, 8, 128), F32),
        V((4, hz, 16, 128), F32), V((8, 128), F32), V((nz, 8, 128), F32),
        V((8, 16, 128), BF16), V((4, 8, 128), F32),
        V((2 * n_pos, 128), F32), V((128, 128), F32),
        V((3, 32, 128), BF16), V((2, 128), F32), V((3, 32, 128), BF16), V((3, 2, 128), F32),
        V((32, 128), BF16), V((2, 128), F32), V((nz, 32, 128), BF16), V((nz, 2, 128), F32),
        V((128, 128), F32), V((2, 4, 32, 128), BF16), V((2, 16, 128), F32),
        V((NY, piece, 32), BF16), V((ny, piece, 32), BF16),
        pltpu.SemaphoreType.DMA((8,)), pltpu.SemaphoreType.DMA, pltpu.SemaphoreType.DMA((17,)),
    ]
    return pl.pallas_call(
        functools.partial(kernel, NZ, NY),
        out_shape=jax.ShapeDtypeStruct((2, 16, piece), BF16),
        in_specs=[pl.BlockSpec(memory_space=pl.ANY)] * 8,
        out_specs=pl.BlockSpec(memory_space=pltpu.VMEM),
        scratch_shapes=scratch,
        compiler_params=pltpu.CompilerParams(
            collective_id=0, has_side_effects=True, vmem_limit_bytes=60 * 2**20),
        name="decode_step",
    )(*args)


def solution(mesh):
    NZ = mesh.shape["ctx"] // (2 * NX)
    return jax.shard_map(
        functools.partial(per_device, NZ, mesh.shape["head"]),
        mesh=mesh,
        in_specs=(
            P(None, None, "ctx"),
            P("ctx", "head"),
            P("ctx", "head"),
            P("ctx", "head"),
            P(None, "head", "ctx", None),
            P(None, "head", "ctx", None),
            P(),
            P("head", "ctx"),
        ),
        out_specs=P(None, None, ("ctx", "head")),
        check_vma=False,
    )
```

```python
import functools
import math

import jax
import jax.numpy as jnp
from jax import lax
from jax.experimental import pallas as pl
from jax.experimental.pallas import tpu as pltpu
from jax.sharding import PartitionSpec as P

F32, BF16 = jnp.float32, jnp.bfloat16
MESH = pl.DeviceIdType.MESH
NX = 4
NEG = -1e30


def dot_t(a, b, **kw):
    return lax.dot_general(a, b, (((1,), (1,)), ((), ())), preferred_element_type=F32, **kw)


def kernel(NZ, NY,
           tok, wq, wk, wv, kc, vc, ln, wo, out,
           tok_v, wq_v, wk_v, wv_v, k_v, v_v, ln_s, wo_v, vt,
           p_oq, p_okv, p_cq, p_ckv, r_cq, r_ckv, s_zq, r_zq, s_xkv, r_xkv, r_xq, s_zkv, r_zkv, q_full, kv_full,
           bias, s_buf, o_buf, s_x2, s_xml, r_x2, r_xml, s_z2, s_zml, r_z2, r_zml,
           o_draft, att, y_buf, s_y, r_y,
           load_sem, send_sem, recv_sem):
    ctx, y = lax.axis_index("ctx"), lax.axis_index("head")
    c = lax.rem(ctx, 2)
    x = lax.rem(ctx // 2, NX)
    z = ctx // (2 * NX)
    o = 1 - c
    n_pos, hz = v_v.shape[1], 8 // NZ

    core_peer = {"ctx": ctx + 1 - 2 * c}
    x_peers = [lax.rem(x + k, NX) for k in (2, 1, 3)]
    x_dev = [{"ctx": (z * NX + xp) * 2 + c} for xp in x_peers]
    far_dev = [{"ctx": (z * NX + xp) * 2 + o} for xp in x_peers]
    z_peers = [lax.rem(z + k, NZ) for k in sorted(range(1, NZ), key=lambda k: -min(k, NZ - k))]
    z_dev = [{"ctx": (zp * NX + x) * 2 + c} for zp in z_peers]
    y_peers = [lax.rem(y + k, NY) for k in sorted(range(1, NY), key=lambda k: -min(k, NY - k))]
    y_dev = [{"head": yp} for yp in y_peers]

    bar = pltpu.get_barrier_semaphore()
    everyone = z_dev + y_dev + x_dev + [core_peer]
    for d in everyone:
        pl.semaphore_signal(bar, inc=1, device_id=d, device_id_type=MESH)

    def load(i, src, dst):
        cp = pltpu.make_async_copy(src, dst, load_sem.at[i])
        cp.start()
        return cp

    ld_tok = load(0, tok, tok_v)
    ld_wq = load(1, wq, wq_v)
    ld_wk = load(2, wk, wk_v)
    ld_wv = load(3, wv, wv_v)
    ld_v = load(4, vc.at[c, 0], v_v.at[0])
    ld_k = load(5, kc.at[c, 0], k_v.at[0:n_pos])
    ld_wo = load(6, wo, wo_v)
    ld_ln = load(7, ln, ln_s)

    pending = []

    def send(ph, src, dst, dev):
        pltpu.make_async_remote_copy(src_ref=src, dst_ref=dst, send_sem=send_sem,
                                     recv_sem=recv_sem.at[ph], device_id=dev, device_id_type=MESH).start()

    def arrive(ph, ref):
        pltpu.make_async_copy(ref, ref, recv_sem.at[ph]).wait()
        pending.append(ref)

    def project(b, dst_q, dst_kv):
        t = tok_v[b]
        q = jnp.dot(t, wq_v[...], preferred_element_type=F32)
        k = jnp.dot(t, wk_v[...], preferred_element_type=F32)
        v = jnp.dot(t, wv_v[...], preferred_element_type=F32)
        for h in range(8):
            dst_q[h] = q[:, 128 * h:128 * h + 128]
        for r in range(2):
            dst_kv[2 * r] = k[8 * r:8 * r + 8]
            dst_kv[2 * r + 1] = v[8 * r:8 * r + 8]

    for cp in (ld_tok, ld_wq, ld_wk, ld_wv):
        cp.wait()
    project(o, p_oq, p_okv)
    project(c, p_cq, p_ckv)
    pl.semaphore_wait(bar, len(everyone))
    send(0, p_oq, r_cq, core_peer)
    send(1, p_okv, r_ckv, core_peer)

    arrive(0, r_cq)
    for i, zp in enumerate(z_peers):
        heads = pl.ds(zp * hz, hz)
        s_zq[i] = p_cq[heads] + r_cq[heads]
        send(2, s_zq.at[i], r_zq.at[i], z_dev[i])
    heads = pl.ds(z * hz, hz)
    qs = p_cq[heads] + r_cq[heads]

    arrive(1, r_ckv)
    for i, xp in enumerate(x_peers):
        s_xkv[i] = p_ckv[xp] + r_ckv[xp]
        send(3, s_xkv.at[i], r_xkv.at[i], x_dev[i])
    kvs = p_ckv[x] + r_ckv[x]

    send(8, vc.at[o, 0], v_v.at[1], core_peer)
    send(9, kc.at[o, 0], k_v.at[n_pos:2 * n_pos], core_peer)

    if NZ > 1:
        arrive(2, r_zq)
        for i in range(NZ - 1):
            qs = qs + r_zq[i]
    r_xq[x] = qs
    for i in range(NX - 1):
        send(4, r_xq.at[x], r_xq.at[x], x_dev[i])

    arrive(3, r_xkv)
    for i in range(NX - 1):
        kvs = kvs + r_xkv[i]
    s_zkv[...] = kvs
    for i in range(NZ - 1):
        send(5, s_zkv, r_zkv.at[i], z_dev[i])

    arrive(4, r_xq.at[0:NX - 1])
    qs = (r_xq[0] + r_xq[1]) + (r_xq[2] + r_xq[3])
    q_full[heads] = (qs * (1.0 / math.sqrt(128.0))).astype(BF16)
    for i in range(NZ - 1):
        send(6, q_full.at[heads], q_full.at[heads], z_dev[i])

    if NZ > 1:
        arrive(5, r_zkv)
        for i in range(NZ - 1):
            kvs = kvs + r_zkv[i]
    kv_full[x] = kvs
    for i in range(NX - 1):
        send(7, kv_full.at[x], kv_full.at[x], x_dev[i])

    vt[128:144] = jnp.ones((16, vt.shape[1]), BF16)

    def transpose_values(half):
        for i in range(4):
            w = n_pos // 4
            vt[0:128, half * n_pos + w * i:half * n_pos + w * (i + 1)] = v_v[half, w * i:w * (i + 1)].T

    ld_ln.wait()
    for half in range(2):
        live = ln_s[c] - (ctx + half * (1 - 2 * c)) * n_pos
        at = lax.broadcasted_iota(jnp.int32, (n_pos, 128), 0)
        bias[half * n_pos:(half + 1) * n_pos] = jnp.where(at < live, 0.0, NEG)
    ld_v.wait()
    transpose_values(0)
    arrive(8, v_v.at[0])
    transpose_values(1)
    ld_k.wait()
    arrive(9, k_v.at[0:n_pos])
    if NZ > 1:
        arrive(6, q_full.at[0:8 - hz])

    q = q_full[...].reshape(128, 128)
    m = jnp.full((8, 128), NEG, F32)
    for n in range(2 * n_pos // 1024):
        rows = slice(1024 * n, 1024 * (n + 1))
        s = dot_t(k_v[rows], q) + bias[rows]
        s_buf[rows] = s
        m = jnp.maximum(m, jnp.max(s.reshape(1024 // 8, 8, 128), axis=0))
    m = jnp.max(m, axis=0, keepdims=True)
    acc = jnp.zeros((144, 128), F32)
    for n in range(2 * n_pos // 512):
        rows = slice(512 * n, 512 * (n + 1))
        w = jnp.exp(s_buf[rows] - m).astype(BF16)
        acc = acc + jnp.dot(vt[:, rows], w, preferred_element_type=F32)
    total = acc[128:129]
    o_buf[...] = acc[0:128]
    s_xml[0:1] = m
    s_xml[1:2] = total
    def chunk(xp):
        return o_buf[pl.ds(pl.multiple_of(xp * 32, 32), 32)]

    for i, xp in enumerate(x_peers):
        s_x2[i] = chunk(xp).astype(BF16)
        send(10, s_x2.at[i], r_x2.at[i], x_dev[i])
        send(11, s_xml, r_xml.at[i], x_dev[i])
    part = chunk(x)

    arrive(7, kv_full.at[0:NX - 1])
    new_k = jnp.concatenate([kv_full[0], kv_full[2]], axis=0)
    new_v = jnp.concatenate([kv_full[1], kv_full[3]], axis=0)
    ds = dot_t(new_k, q.astype(F32), precision=lax.Precision.HIGHEST)
    lane = lax.broadcasted_iota(jnp.int32, (16, 128), 1)
    u = lax.broadcasted_iota(jnp.int32, (16, 128), 0)
    ds = jnp.where(u <= lane % 16, ds, NEG)
    dm = jnp.max(ds, axis=0, keepdims=True)
    dw = jnp.exp(ds - dm)
    dl = jnp.sum(dw, axis=0, keepdims=True)
    o_draft[...] = lax.dot_general(new_v, dw, (((0,), (0,)), ((), ())), preferred_element_type=F32,
                                   precision=lax.Precision.HIGHEST)
    d_part = o_draft[pl.ds(pl.multiple_of(x * 32, 32), 32)]

    def combine(parts):
        top = functools.reduce(jnp.maximum, [m for m, _, _ in parts])
        tot, acc = 0.0, 0.0
        for m, l, a in parts:
            f = jnp.exp(m - top)
            tot = tot + f * l
            acc = acc + f * a
        return top, tot, acc

    arrive(10, r_x2)
    arrive(11, r_xml)
    m, total, part = combine(
        [(m, total, part)] + [(r_xml[i, 0:1], r_xml[i, 1:2], r_x2[i].astype(F32)) for i in range(NX - 1)])
    s_z2[...] = part.astype(BF16)
    s_zml[0:1] = m
    s_zml[1:2] = total
    for i in range(NZ - 1):
        send(12, s_z2, r_z2.at[i], z_dev[i])
        send(13, s_zml, r_zml.at[i], z_dev[i])
    ld_wo.wait()
    if NZ > 1:
        arrive(12, r_z2)
        arrive(13, r_zml)
    _, total, part = combine(
        [(m, total, part), (dm, dl, d_part)]
        + [(r_zml[i, 0:1], r_zml[i, 1:2], r_z2[i].astype(F32)) for i in range(NZ - 1)])
    att[c, x] = (part / total).astype(BF16)
    for d in far_dev:
        send(15, att.at[c, x], att.at[c, x], d)
    for d in x_dev:
        send(14, att.at[c, x], att.at[c, x], d)
    send(15, att.at[c, x], att.at[c, x], core_peer)
    arrive(14, att.at[0, 0:NX - 1])

    def mix(b):
        a = att[b].reshape(128, 128).T
        a = jnp.concatenate([a[16 * h:16 * h + 16] for h in range(8)], axis=1)
        y_buf[b] = jnp.dot(a, wo_v[...], preferred_element_type=F32)

    mix(c)
    arrive(15, att.at[0])
    mix(o)
    yt = y_buf[...].reshape(32, 128).T.astype(BF16)
    s_y[...] = yt.reshape(s_y.shape)
    for i in range(NY - 1):
        send(16, s_y.at[y_peers[i]], r_y.at[i], y_dev[i])
    ys = s_y[y].astype(F32)
    if NY > 1:
        arrive(16, r_y)
        for i in range(NY - 1):
            ys = ys + r_y[i].astype(F32)
    out[...] = ys.T.astype(BF16).reshape(out.shape)

    for ref in pending:
        pltpu.make_async_copy(ref, ref, send_sem).wait()


def per_device(NZ, NY, *args):
    tok, wq, wk, wv, kc, vc, ln, wo = args
    n_pos, piece, hz = kc.shape[2], wo.shape[1] // NY, 8 // NZ
    nz, ny = max(NZ - 1, 1), max(NY - 1, 1)
    V = pltpu.VMEM
    scratch = [
        V(tok.shape, BF16), V(wq.shape, BF16), V(wk.shape, BF16), V(wv.shape, BF16),
        V((2 * n_pos, 128), BF16), V((2, n_pos, 128), BF16), pltpu.SMEM((2,), jnp.int32), V(wo.shape, BF16),
        V((144, 2 * n_pos), BF16),
        V((8, 16, 128), F32), V((4, 8, 128), F32), V((8, 16, 128), F32), V((4, 8, 128), F32),
        V((8, 16, 128), F32), V((4, 8, 128), F32),
        V((nz, hz, 16, 128), F32), V((nz, hz, 16, 128), F32), V((3, 8, 128), F32), V((3, 8, 128), F32),
        V((4, hz, 16, 128), F32), V((8, 128), F32), V((nz, 8, 128), F32),
        V((8, 16, 128), BF16), V((4, 8, 128), F32),
        V((2 * n_pos, 128), F32), V((2 * n_pos, 128), F32), V((128, 128), F32),
        V((3, 32, 128), BF16), V((2, 128), F32), V((3, 32, 128), BF16), V((3, 2, 128), F32),
        V((32, 128), BF16), V((2, 128), F32), V((nz, 32, 128), BF16), V((nz, 2, 128), F32),
        V((128, 128), F32), V((2, 4, 32, 128), BF16), V((2, 16, 128), F32),
        V((NY, piece, 32), BF16), V((ny, piece, 32), BF16),
        pltpu.SemaphoreType.DMA((8,)), pltpu.SemaphoreType.DMA, pltpu.SemaphoreType.DMA((17,)),
    ]
    return pl.pallas_call(
        functools.partial(kernel, NZ, NY),
        out_shape=jax.ShapeDtypeStruct((2, 16, piece), BF16),
        in_specs=[pl.BlockSpec(memory_space=pl.ANY)] * 8,
        out_specs=pl.BlockSpec(memory_space=pltpu.VMEM),
        scratch_shapes=scratch,
        compiler_params=pltpu.CompilerParams(
            collective_id=0, has_side_effects=True, vmem_limit_bytes=60 * 2**20),
        name="decode_step",
    )(*args)


def solution(mesh):
    NZ = mesh.shape["ctx"] // (2 * NX)
    return jax.shard_map(
        functools.partial(per_device, NZ, mesh.shape["head"]),
        mesh=mesh,
        in_specs=(
            P(None, None, "ctx"),
            P("ctx", "head"),
            P("ctx", "head"),
            P("ctx", "head"),
            P(None, "head", "ctx", None),
            P(None, "head", "ctx", None),
            P(),
            P("head", "ctx"),
        ),
        out_specs=P(None, None, ("ctx", "head")),
        check_vma=False,
    )
```
